32 devices in a mesh: grp: 2 (over y), seq: 16 (over z, x, core).
Axes of the slice: x: 2, y: 2, z: 4, core: 2. Of those that a mesh axis runs over, the one named last changes fastest.
Arguments:
- normed_input: bfloat16 [4096, 8192], P(('grp', 'seq')), parts along dimension 0, may hold values from -6 to 6
- base_projection_weight: bfloat16 [4096, 1280], P(('grp', 'seq')), parts along dimension 0, may hold values from -24 to 24
- adapter_down_pool: bfloat16 [16, 192, 8192], P('seq'), may hold values from -0.0625 to 0.0625
- adapter_up_pool: bfloat16 [16, 64, 1280], P('seq'), may hold values from -0.75 to 0.75
- output_down_pool: bfloat16 [16, 64, 1024], P('seq'), may hold values from -0.1875 to 0.1875
- output_up_pool: bfloat16 [16, 64, 8192], P('seq'), may hold values from -0.75 to 0.75
- request_adapter_ids: int32 [4], P('grp'), parts along dimension 0, may hold values from 0 to 15, as said below
- holder: int32 [16], replicated, may hold values from 0 to 15, each once
- segment_adapter_entry: int32 [32], P(('grp', 'seq')), parts along dimension 0, may hold values from 0 to 1
Outputs:
- attended: bfloat16 [4096, 1024], P(('grp', 'seq')), parts along dimension 0
- output_delta: bfloat16 [4096, 8192], P(('grp', 'seq')), parts along dimension 0
The draws below stay inside these ranges and needn't reach their ends.
There are 2 independent parts, one for each index of `grp`. The reference program is written for one: setup_inputs(seed, part) draws one part's arguments, and reference() takes and returns one part's arrays. A program takes and returns all parts, laid end to end along the dimension named above; an argument that names none is the same for every part. Nothing has to cross between parts.
Inputs may be any that keep to these rules, and one draw needn't show every extreme that they name: `request_adapter_ids`: 2 distinct adapter ids; the largest is 15.
All inputs are finite; a program needn't handle non-finite values.
Results may differ from the reference program's by a relative error of at most 0.012.
The reference program's roundings to bfloat16 on the way count: a program that leaves them out, or rounds other values in their place, can miss the bound.
Values may be sent and summed in bfloat16 or wider, within the bound.
A program may use at most 64 MiB of HBM per device.

```python
import math
import jax
import jax.numpy as jnp
from jax import lax

MODEL_WIDTH = 8192
HEAD_SIZE = 128
QUERY_PER_GROUP = 8
ADAPTER_RANK = 64
SEG_LEN = 128
USED = 2
PROJECT_COLUMNS = 1280
ADAPTER_SLOTS = 16
S = 2048
SEGS = 16


def draw_normed_input(key, part):
    key = jax.random.fold_in(key, 11)
    drawn_rows = jnp.clip(jax.random.normal(key, (S, MODEL_WIDTH), jnp.float32), -6.0, 6.0)
    return drawn_rows.astype(jnp.bfloat16)


def draw_base_projection_weight(key, part):
    key = jax.random.fold_in(key, 12)
    base_rows = jnp.clip(jax.random.normal(key, (S, PROJECT_COLUMNS), jnp.float32), -6.0, 6.0)
    return base_rows.astype(jnp.bfloat16)


def draw_request_adapter_ids(key, part):
    key = jax.random.fold_in(key, 13)
    others = jax.random.permutation(jax.random.fold_in(key, 1), ADAPTER_SLOTS - 1)[:USED].astype(jnp.int32)
    largest_place = jnp.asarray(part, jnp.int32) % USED
    entries = jnp.arange(USED, dtype=jnp.int32)
    other_index = jnp.where(entries < largest_place, entries, entries - 1)
    other_index = jnp.clip(other_index, 0, USED - 1)
    listed = jnp.where(entries == largest_place, ADAPTER_SLOTS - 1, others[other_index])
    return listed.astype(jnp.int32)


def plant(values, stream_key, smallest, high):
    longest = values.shape.index(max(values.shape))
    spots = []
    for shift in (0, 1):
        where = [jax.random.randint(jax.random.fold_in(stream_key, axis), (), 0, length) for axis, length in enumerate(values.shape)]
        where[longest] = (where[longest] + shift) % values.shape[longest]
        spots.append(tuple(where))
    return values.at[spots[0]].set(smallest).at[spots[1]].set(high)


def level_of(own_key, extent, shards, smallest, largest):
    def one(dim, blocks):
        steps = jax.random.uniform(jax.random.fold_in(jax.random.fold_in(own_key, 6), dim), (blocks,), jnp.float32, smallest / len(shards), largest / len(shards))
        return jnp.repeat(jnp.exp(steps), extent[dim] // blocks).reshape((-1,) + (1,) * (len(extent) - dim - 1))

    loudness = one(*shards[0])
    for cut in shards[1:]:
        loudness = loudness * one(*cut)
    return loudness


def centred(own_key, shape, deviation, limit, split=(), held_as=jnp.bfloat16):
    loudness = level_of(own_key, shape, split, -0.22, 0.18) if split else 1.0
    result = jax.random.normal(own_key, shape, jnp.float32) * deviation * loudness
    return jnp.minimum(jnp.maximum(result, -limit), limit).astype(held_as)


def setup_inputs(seed: int = 0, part: int = 0) -> dict:
    seeds = jax.random.split(jax.random.key(seed), 10)
    own_keys = jax.random.split(jax.random.fold_in(seeds[9], part), 10)
    normed_input = draw_normed_input(jax.random.fold_in(jax.random.fold_in(seeds[9], part), 71), part)
    base_projection_weight = draw_base_projection_weight(jax.random.fold_in(jax.random.fold_in(seeds[9], part), 71), part)
    adapter_down_pool = centred(seeds[2], (ADAPTER_SLOTS, 3 * ADAPTER_RANK, MODEL_WIDTH), MODEL_WIDTH ** -0.5, 0.0625, ((0, 16),))
    adapter_up_pool = centred(seeds[3], (ADAPTER_SLOTS, ADAPTER_RANK, PROJECT_COLUMNS), ADAPTER_RANK ** -0.5, 0.75, ((0, 16),))
    output_down_pool = centred(seeds[4], (ADAPTER_SLOTS, ADAPTER_RANK, QUERY_PER_GROUP * HEAD_SIZE), (QUERY_PER_GROUP * HEAD_SIZE) ** -0.5, 0.1875, ((0, 16),))
    output_up_pool = centred(seeds[5], (ADAPTER_SLOTS, ADAPTER_RANK, MODEL_WIDTH), ADAPTER_RANK ** -0.5, 0.75, ((0, 16),))
    request_adapter_ids = draw_request_adapter_ids(jax.random.fold_in(jax.random.fold_in(seeds[9], part), 71), part)
    holder = jax.random.permutation(seeds[7], ADAPTER_SLOTS).astype(jnp.int32)
    segment_adapter_entry = plant(jax.random.randint(own_keys[8], (SEGS,), 0, USED), jax.random.fold_in(own_keys[8], 1), 0, USED - 1).astype(jnp.int32)
    return dict(normed_input=normed_input, base_projection_weight=base_projection_weight, adapter_down_pool=adapter_down_pool, adapter_up_pool=adapter_up_pool, output_down_pool=output_down_pool, output_up_pool=output_up_pool, request_adapter_ids=request_adapter_ids, holder=holder, segment_adapter_entry=segment_adapter_entry)


rope_base = 1000000.0


def rope_tables(positions, head_width):
    half_width = head_width // 2
    frequency = jnp.exp(jnp.arange(half_width, dtype=jnp.float32) * (-2.0 * math.log(rope_base) / head_width))
    angles = positions.astype(jnp.float32)[:, None] * frequency[None, :]
    return jnp.cos(angles), jnp.sin(angles)


def rotate(vectors, cosine, sine_table):
    half_width = vectors.shape[-1] // 2
    first_half = vectors[..., :half_width]
    second_half = vectors[..., half_width:]
    return jnp.concatenate([first_half * cosine - second_half * sine_table, second_half * cosine + first_half * sine_table], -1)


def reference(normed_input, base_projection_weight, adapter_down_pool, adapter_up_pool, output_down_pool, output_up_pool, request_adapter_ids, holder, segment_adapter_entry):
    query_width = QUERY_PER_GROUP * HEAD_SIZE
    pool_slots = holder[request_adapter_ids]
    segment_slots = pool_slots[segment_adapter_entry]

    def adapt_inputs(operands):
        token_rows, adapter_slot_index = operands
        down_weight = adapter_down_pool[adapter_slot_index]
        up_weight = adapter_up_pool[adapter_slot_index]
        reduced_rank_rows = jnp.dot(token_rows, down_weight.T, preferred_element_type=jnp.float32).astype(jnp.bfloat16)
        delta_query = jnp.dot(reduced_rank_rows[:, :ADAPTER_RANK], up_weight[:, :query_width], preferred_element_type=jnp.float32)
        delta_key = jnp.dot(reduced_rank_rows[:, ADAPTER_RANK:2 * ADAPTER_RANK], up_weight[:, query_width:query_width + HEAD_SIZE], preferred_element_type=jnp.float32)
        delta_value = jnp.dot(reduced_rank_rows[:, 2 * ADAPTER_RANK:], up_weight[:, query_width + HEAD_SIZE:], preferred_element_type=jnp.float32)
        return jnp.concatenate([delta_query, delta_key, delta_value], 1)

    delta_qkv = lax.map(adapt_inputs, (normed_input.reshape(SEGS, SEG_LEN, MODEL_WIDTH), segment_slots)).reshape(S, PROJECT_COLUMNS)
    combined = base_projection_weight.astype(jnp.float32) + delta_qkv
    positions = jnp.arange(S)
    cosine, sine_table = rope_tables(positions, HEAD_SIZE)
    queries = rotate(combined[:, :query_width].reshape(S, QUERY_PER_GROUP, HEAD_SIZE), cosine[:, None, :], sine_table[:, None, :]).astype(jnp.bfloat16)
    key_rows = rotate(combined[:, query_width:query_width + HEAD_SIZE], cosine, sine_table).astype(jnp.bfloat16)
    value_rows = combined[:, query_width + HEAD_SIZE:].astype(jnp.bfloat16)
    block_rows = math.gcd(S, 512)
    key_wide = key_rows.astype(jnp.float32)
    value_wide = value_rows.astype(jnp.float32)
    scale = HEAD_SIZE ** -0.5

    def attend(operands):
        query_block, block_start = operands
        scores = jnp.einsum("qhd,kd->hqk", query_block.astype(jnp.float32), key_wide) * scale
        visible = jnp.arange(S)[None, :] <= (block_start + jnp.arange(block_rows))[:, None]
        scores = jnp.where(visible[None], scores, -1e30)
        maxima = jnp.max(scores, -1, keepdims=True)
        weights = jnp.where(visible[None], jnp.exp(scores - maxima), 0.0)
        totals = jnp.sum(weights, -1)
        rounded = lax.optimization_barrier(weights.astype(jnp.bfloat16))
        summed = jnp.einsum("hqk,kd->qhd", rounded.astype(jnp.float32), value_wide)
        return (summed / totals.T[:, :, None]).reshape(block_rows, query_width).astype(jnp.bfloat16)

    block_starts = jnp.arange(S // block_rows) * block_rows
    attended = lax.map(attend, (queries.reshape(S // block_rows, block_rows, QUERY_PER_GROUP, HEAD_SIZE), block_starts)).reshape(S, query_width)

    def adapt_output(operands):
        attention_rows, adapter_slot_index = operands
        reduced_rank_rows = jnp.dot(attention_rows, output_down_pool[adapter_slot_index].T, preferred_element_type=jnp.float32).astype(jnp.bfloat16)
        return jnp.dot(reduced_rank_rows, output_up_pool[adapter_slot_index], preferred_element_type=jnp.float32).astype(jnp.bfloat16)

    output_delta = lax.map(adapt_output, (attended.reshape(SEGS, SEG_LEN, query_width), segment_slots)).reshape(S, MODEL_WIDTH)
    return attended, output_delta
```

```python
from functools import partial
import math

import jax
import jax.numpy as jnp
from jax import lax
from jax.experimental import pallas as pl
from jax.experimental.pallas import tpu as pltpu
from jax.sharding import PartitionSpec as P

HEAD_SIZE = 128
QUERY_PER_GROUP = 8
ADAPTER_RANK = 64
USED = 2

rope_base = 1000000.0

MESH = pl.DeviceIdType.MESH
BLOCK = 1024
LANE_ROWS = 16
SKEW = 2
OWN_CHUNKS = 35
ALL_CHUNKS = 53
QUARTER = 80


def chip_grid(chips):
    columns = 1
    while 2 * (2 * columns) ** 2 <= chips:
        columns *= 2
    return columns, chips // columns


def path_position(path, x, z, core, columns, rows):
    if path == 0:
        z = z + core * (rows - 1 - 2 * z)
        return x * rows + z + (x % 2) * (rows - 1 - 2 * z)
    x = x + core * (columns - 1 - 2 * x)
    return z * columns + x + (z % 2) * (columns - 1 - 2 * x)


def path_device(path, position, core, columns, rows):
    if path == 0:
        x = position // rows
        z = position % rows
        z = z + (x % 2) * (rows - 1 - 2 * z)
        z = z + core * (rows - 1 - 2 * z)
    else:
        z = position // columns
        x = position % columns
        x = x + (z % 2) * (columns - 1 - 2 * x)
        x = x + core * (columns - 1 - 2 * x)
    return (z * columns + x) * 2 + core


def chunk_place(k, quarter, grp):
    shared = k // OWN_CHUNKS
    kk = k - OWN_CHUNKS * shared
    group = kk // 8
    block = kk % 8
    narrow = shared * (group // 2)
    row = (
        QUARTER * quarter
        + LANE_ROWS * group
        + shared * (1 - group // 2) * (32 * grp)
        + narrow * 32
    )
    column = BLOCK * (block + narrow * 2 * grp)
    return shared, pl.multiple_of(row, LANE_ROWS), pl.multiple_of(column, BLOCK)


def fetch_kernel(
    seq_size,
    slots,
    ids_ref,
    holder_ref,
    entry_ref,
    x_ref,
    down_ref,
    up_ref,
    out_down_ref,
    out_up_ref,
    shrunk_ref,
    narrow_ref,
    wide_ref,
    own,
    mate_rows,
    moving,
    whole,
    load_sem,
    mate_send,
    mate_recv,
    chain_send,
    chain_recv,
    post_send,
    post_recv,
    cross_send,
    cross_recv,
):
    chips = seq_size // 2
    columns, rows = chip_grid(chips)
    grp = lax.axis_index("grp")
    me = lax.axis_index("seq")
    core = me % 2
    chip = me // 2
    x = chip % columns
    z = chip // columns
    mate = me + 1 - 2 * core
    other = 1 - grp
    positions = [path_position(j, x, z, core, columns, rows) for j in range(2)]

    def device_at(j, position):
        clipped = jnp.clip(position, 0, chips - 1)
        return path_device(j, clipped, core, columns, rows)

    following = [device_at(j, positions[j] + 1) for j in range(2)]
    preceding = [device_at(j, positions[j] - 1) for j in range(2)]

    loads = []
    for q in range(4):
        wide = down_ref.at[0, pl.ds(64 * q, 64)] if q < 3 else out_up_ref.at[0]
        loads.append((wide, own.at[pl.ds(QUARTER * q, 64)]))
        loads.append(
            (
                up_ref.at[0, pl.ds(16 * q, 16)],
                own.at[pl.ds(QUARTER * q + 64, 16), pl.ds(0, 1280)],
            )
        )
        loads.append(
            (
                out_down_ref.at[0, pl.ds(16 * q, 16)],
                own.at[pl.ds(QUARTER * q + 64, 16), pl.ds(1280, 1024)],
            )
        )
    loads = [
        pltpu.make_async_copy(source, target, load_sem.at[i])
        for i, (source, target) in enumerate(loads)
    ]
    for load in loads:
        load.start()
    for q in range(4):
        own[pl.ds(QUARTER * q + 64, 16), pl.ds(2304, 1792)] = jnp.zeros((16, 1792), jnp.bfloat16)

    barrier = pltpu.get_barrier_semaphore()

    def greet(device):
        pl.semaphore_signal(barrier, inc=1, device_id=device, device_id_type=MESH)

    greet((grp, mate))
    greet((other, me))
    greet((other, mate))
    expected = 3
    for j in range(2):

        @pl.when(positions[j] > 0)
        def _():
            greet((grp, preceding[j]))

        @pl.when(positions[j] < chips - 1)
        def _():
            greet((grp, following[j]))

        expected = expected + jnp.minimum(positions[j], 1)
        expected = expected + jnp.minimum(chips - 1 - positions[j], 1)

    rest = jnp.clip(ids_ref[0] + ids_ref[1] - (slots - 1), 0, slots - 1)
    owners = [holder_ref[rest], holder_ref[slots - 1]]
    mine = [jnp.where(owner == me, 1, 0) for owner in owners]
    mates = [jnp.where(owner == mate, 1, 0) for owner in owners]
    ahead = []
    for j in range(2):
        per_path = []
        for owner in owners:
            owner_chip = owner // 2
            place = path_position(
                j, owner_chip % columns, owner_chip // columns, core, columns, rows
            )
            per_path.append(jnp.where(place <= positions[j], 1, 0))
        ahead.append(per_path)
    picked = ids_ref[entry_ref[0]] == slots - 1

    pl.semaphore_wait(barrier, expected)
    for load in loads:
        load.wait()

    def mate_copy(j, group):
        source = 2 * (1 - core) + j
        return pltpu.make_async_remote_copy(
            src_ref=own.at[pl.ds(pl.multiple_of(QUARTER * source + 16 * group, 16), 16)],
            dst_ref=mate_rows.at[pl.ds(pl.multiple_of(QUARTER * j + 16 * group, 16), 16)],
            send_sem=mate_send,
            recv_sem=mate_recv.at[j * 5 + group],
            device_id=(grp, mate),
            device_id_type=MESH,
        )

    for group in range(5):
        for j in range(2):
            mate_copy(j, group).start()

    def chunk(d, j, k):
        return moving.at[d, j, pl.ds(pl.multiple_of(LANE_ROWS * k, LANE_ROWS), LANE_ROWS)]

    def chain_copy(d, j, k):
        return pltpu.make_async_remote_copy(
            src_ref=chunk(d, j, k),
            dst_ref=chunk(d, j, k),
            send_sem=chain_send.at[2 * d + j],
            recv_sem=chain_recv.at[(2 * d + j) * ALL_CHUNKS + k],
            device_id=(grp, following[j] if d == 0 else preceding[j]),
            device_id_type=MESH,
        )

    def post_copy(target, row, column, send_sem, recv_sem):
        piece = whole.at[pl.ds(row, LANE_ROWS), pl.ds(column, BLOCK)]
        return pltpu.make_async_remote_copy(
            src_ref=piece,
            dst_ref=piece,
            send_sem=send_sem,
            recv_sem=recv_sem,
            device_id=target,
            device_id_type=MESH,
        )

    def step(t, carry):
        @pl.when(jnp.logical_and(t % 8 == 0, t < 40))
        def _():
            for j in range(2):
                piece = mate_rows.at[pl.ds(0, 16)]
                pltpu.make_async_copy(piece, piece, mate_recv.at[j * 5 + t // 8]).wait()

        for j in range(2):
            for d in range(2):
                hops = positions[j] if d == 0 else chips - 1 - positions[j]
                k = t - SKEW * hops

                @pl.when(jnp.logical_and(k >= 0, k < ALL_CHUNKS))
                def _():
                    @pl.when(hops > 0)
                    def _():
                        chain_copy(d, j, k).wait_recv()

                    shared, row, column = chunk_place(k, 2 * core + j, grp)
                    mine_now = mine[0] + shared * (mine[1] - mine[0])
                    mate_now = mates[0] + shared * (mates[1] - mates[0])
                    here = own[pl.ds(row, LANE_ROWS), pl.ds(column, BLOCK)]
                    mate_row = pl.multiple_of(row - 2 * QUARTER * core, LANE_ROWS)
                    there = mate_rows[pl.ds(mate_row, LANE_ROWS), pl.ds(column, BLOCK)]
                    slot = pl.ds(pl.multiple_of(LANE_ROWS * k, LANE_ROWS), LANE_ROWS)
                    passed = moving[d, j, slot]
                    passed = lax.select_n(mate_now == 1, passed, there)
                    moving[d, j, slot] = lax.select_n(mine_now == 1, passed, here)

                    @pl.when(hops < chips - 1)
                    def _():
                        chain_copy(d, j, k).start()

            late = jnp.maximum(positions[j], chips - 1 - positions[j])
            done = t - SKEW * late

            @pl.when(jnp.logical_and(done >= 0, done < ALL_CHUNKS))
            def _():
                shared, row, column = chunk_place(done, 2 * core + j, grp)
                row = pl.multiple_of(row + 4 * QUARTER * shared, LANE_ROWS)
                slot = pl.ds(pl.multiple_of(LANE_ROWS * done, LANE_ROWS), LANE_ROWS)
                ahead_now = ahead[j][0] + shared * (ahead[j][1] - ahead[j][0])
                whole[pl.ds(row, LANE_ROWS), pl.ds(column, BLOCK)] = lax.select_n(
                    ahead_now == 1, moving[1, j, slot], moving[0, j, slot]
                )
                post_copy((grp, mate), row, column, post_send, post_recv).start()

                @pl.when(done >= OWN_CHUNKS)
                def _():
                    post_copy(
                        (other, me), row, column, cross_send.at[0], cross_recv.at[0]
                    ).start()
                    post_copy(
                        (other, mate), row, column, cross_send.at[1], cross_recv.at[1]
                    ).start()

        return carry

    lax.fori_loop(0, ALL_CHUNKS + SKEW * (chips - 1), step, 0)

    def drain(ref, sem):
        pltpu.make_async_copy(ref, ref, sem).wait()

    both = moving.at[0]
    cross = moving.at[0, :, pl.ds(0, LANE_ROWS * (ALL_CHUNKS - OWN_CHUNKS))]
    drain(both, post_recv)
    for i in range(2):
        drain(cross, cross_recv.at[i])

    total = jnp.zeros((x_ref.shape[0], 3 * ADAPTER_RANK), jnp.float32)

    def shrink(block, total):
        at = pl.ds(pl.multiple_of(block * BLOCK, BLOCK), BLOCK)
        parts = [
            lax.select_n(
                picked,
                whole[pl.ds(QUARTER * q, 64), at],
                whole[pl.ds(QUARTER * (4 + q), 64), at],
            )
            for q in range(3)
        ]
        return total + lax.dot_general(
            x_ref[:, at],
            jnp.concatenate(parts, 0),
            (((1,), (1,)), ((), ())),
            preferred_element_type=jnp.float32,
        )

    total = lax.fori_loop(0, x_ref.shape[1] // BLOCK, shrink, total)
    shrunk_ref[...] = total.astype(jnp.bfloat16)
    for q in range(4):
        at = pl.ds(0, 2304)
        narrow_ref[pl.ds(16 * q, 16), :] = lax.select_n(
            picked,
            whole[pl.ds(QUARTER * q + 64, 16), at],
            whole[pl.ds(QUARTER * (4 + q) + 64, 16), at],
        )

    def copy_wide(block, carry):
        at = pl.ds(pl.multiple_of(block * BLOCK, BLOCK), BLOCK)
        wide_ref[:, at] = lax.select_n(
            picked,
            whole[pl.ds(QUARTER * 3, 64), at],
            whole[pl.ds(QUARTER * 7, 64), at],
        )
        return carry

    lax.fori_loop(0, wide_ref.shape[1] // BLOCK, copy_wide, 0)

    drain(mate_rows, mate_send)
    for j in range(2):
        for d in range(2):
            hops = positions[j] if d == 0 else chips - 1 - positions[j]

            @pl.when(hops < chips - 1)
            def _():
                drain(moving.at[d, j], chain_send.at[2 * d + j])

    drain(both, post_send)
    for i in range(2):
        drain(cross, cross_send.at[i])


def rope_tables(positions, head_width):
    half_width = head_width // 2
    frequency = jnp.exp(
        jnp.arange(half_width, dtype=jnp.float32) * (-2.0 * math.log(rope_base) / head_width)
    )
    angles = positions.astype(jnp.float32)[:, None] * frequency[None, :]
    return (jnp.cos(angles), jnp.sin(angles))


def rotate(vectors, cosine, sine_table):
    half_width = vectors.shape[-1] // 2
    first_half = vectors[..., :half_width]
    second_half = vectors[..., half_width:]
    return jnp.concatenate(
        [
            first_half * cosine - second_half * sine_table,
            second_half * cosine + first_half * sine_table,
        ],
        -1,
    )


def absorb(states, queries, positions, key_block, value_block, key_start):
    maxima, totals, summed = states
    scores = jnp.einsum(
        "qhd,kd->hqk", queries, key_block, preferred_element_type=jnp.float32
    ) * HEAD_SIZE ** (-0.5)
    visible = (key_start + jnp.arange(key_block.shape[0], dtype=jnp.int32))[None, :] <= positions[
        :, None
    ]
    scores = jnp.where(visible[None], scores, -1e30)
    new_maxima = jnp.maximum(maxima, jnp.max(scores, -1))
    weights = jnp.where(visible[None], jnp.exp(scores - new_maxima[:, :, None]), 0.0)
    rescale = jnp.exp(maxima - new_maxima)
    totals = totals * rescale + jnp.sum(weights, -1)
    summed = summed * rescale[:, :, None] + jnp.einsum(
        "hqk,kd->hqd", weights.astype(jnp.bfloat16), value_block, preferred_element_type=jnp.float32
    )
    return (new_maxima, totals, summed)


def shards(
    seq_size,
    normed_input,
    base_projection_weight,
    adapter_down_pool,
    adapter_up_pool,
    output_down_pool,
    output_up_pool,
    request_adapter_ids,
    holder,
    segment_adapter_entry,
):
    tok_rows, width = normed_input.shape
    query_width = QUERY_PER_GROUP * HEAD_SIZE
    slots = holder.shape[0]
    in_smem = pl.BlockSpec(memory_space=pltpu.SMEM)
    in_vmem = pl.BlockSpec(memory_space=pltpu.VMEM)
    in_any = pl.BlockSpec(memory_space=pl.ANY)
    bf16 = jnp.bfloat16
    reduced_rank_rows, narrow, out_up = pl.pallas_call(
        partial(fetch_kernel, seq_size, slots),
        out_shape=(
            jax.ShapeDtypeStruct((tok_rows, 3 * ADAPTER_RANK), bf16),
            jax.ShapeDtypeStruct((ADAPTER_RANK, 2304), bf16),
            jax.ShapeDtypeStruct((ADAPTER_RANK, width), bf16),
        ),
        in_specs=[in_smem] * 3 + [in_vmem] + [in_any] * 4,
        out_specs=(in_vmem, in_vmem, in_vmem),
        scratch_shapes=[
            pltpu.VMEM((4 * QUARTER, width), bf16),
            pltpu.VMEM((2 * QUARTER, width), bf16),
            pltpu.VMEM((2, 2, LANE_ROWS * ALL_CHUNKS, BLOCK), bf16),
            pltpu.VMEM((8 * QUARTER, width), bf16),
            pltpu.SemaphoreType.DMA((12,)),
            pltpu.SemaphoreType.DMA,
            pltpu.SemaphoreType.DMA((10,)),
            pltpu.SemaphoreType.DMA((4,)),
            pltpu.SemaphoreType.DMA((4 * ALL_CHUNKS,)),
            pltpu.SemaphoreType.DMA,
            pltpu.SemaphoreType.DMA,
            pltpu.SemaphoreType.DMA((2,)),
            pltpu.SemaphoreType.DMA((2,)),
        ],
        compiler_params=pltpu.CompilerParams(
            collective_id=0, has_side_effects=True, vmem_limit_bytes=48 * 1024 * 1024
        ),
        name="fetch",
    )(
        request_adapter_ids,
        holder,
        segment_adapter_entry,
        normed_input,
        adapter_down_pool,
        adapter_up_pool,
        output_down_pool,
        output_up_pool,
    )
    up_weight = narrow[:, : query_width + 2 * HEAD_SIZE]
    out_down = narrow[:, query_width + 2 * HEAD_SIZE :]
    delta_query = jnp.dot(
        reduced_rank_rows[:, :ADAPTER_RANK],
        up_weight[:, :query_width],
        preferred_element_type=jnp.float32,
    )
    delta_key = jnp.dot(
        reduced_rank_rows[:, ADAPTER_RANK : 2 * ADAPTER_RANK],
        up_weight[:, query_width : query_width + HEAD_SIZE],
        preferred_element_type=jnp.float32,
    )
    delta_value = jnp.dot(
        reduced_rank_rows[:, 2 * ADAPTER_RANK :],
        up_weight[:, query_width + HEAD_SIZE :],
        preferred_element_type=jnp.float32,
    )
    deltas = jnp.concatenate([delta_query, delta_key, delta_value], 1)
    combined = base_projection_weight.astype(jnp.float32) + deltas
    device_index = lax.axis_index("seq")
    positions = device_index * tok_rows + jnp.arange(tok_rows, dtype=jnp.int32)
    cosine, sine_table = rope_tables(positions, HEAD_SIZE)
    queries = rotate(
        combined[:, :query_width].reshape(tok_rows, QUERY_PER_GROUP, HEAD_SIZE),
        cosine[:, None, :],
        sine_table[:, None, :],
    ).astype(jnp.bfloat16)
    key_rows = rotate(
        combined[:, query_width : query_width + HEAD_SIZE], cosine, sine_table
    ).astype(jnp.bfloat16)
    value_rows = combined[:, query_width + HEAD_SIZE :].astype(jnp.bfloat16)
    initial = (
        jnp.full((QUERY_PER_GROUP, tok_rows), -1e30, jnp.float32),
        jnp.zeros((QUERY_PER_GROUP, tok_rows), jnp.float32),
        jnp.zeros((QUERY_PER_GROUP, tok_rows, HEAD_SIZE), jnp.float32),
    )
    pair = lax.all_gather(
        jnp.concatenate([key_rows, value_rows], 1), "seq", axis=0, tiled=True
    )
    piece_rows = pair.shape[0]
    block_rows = math.gcd(piece_rows, 512)

    def one_block(block_index, states):
        local_start = block_index * block_rows
        block = lax.dynamic_slice_in_dim(pair, local_start, block_rows, 0)
        return lax.cond(
            local_start <= positions[-1],
            partial(
                absorb,
                queries=queries,
                positions=positions,
                key_block=block[:, :HEAD_SIZE],
                value_block=block[:, HEAD_SIZE:],
                key_start=local_start,
            ),
            lambda states: states,
            states,
        )

    maxima, totals, summed = lax.fori_loop(0, piece_rows // block_rows, one_block, initial)
    normalized = (summed / totals[:, :, None]).transpose(1, 0, 2)
    attended = normalized.reshape(tok_rows, query_width).astype(jnp.bfloat16)
    reduced_out_rows = lax.dot_general(
        attended, out_down, (((1,), (1,)), ((), ())), preferred_element_type=jnp.float32
    ).astype(jnp.bfloat16)
    out_rows = jnp.dot(reduced_out_rows, out_up, preferred_element_type=jnp.float32).astype(
        jnp.bfloat16
    )
    return (attended, out_rows)


def solution(mesh):
    in_specs = (
        P(("grp", "seq"), None),
        P(("grp", "seq"), None),
        P("seq", None, None),
        P("seq", None, None),
        P("seq", None, None),
        P("seq", None, None),
        P("grp"),
        P(),
        P(("grp", "seq")),
    )
    out_specs = (P(("grp", "seq"), None), P(("grp", "seq"), None))
    return jax.shard_map(
        partial(shards, mesh.shape["seq"]),
        mesh=mesh,
        in_specs=in_specs,
        out_specs=out_specs,
        check_vma=False,
    )
```

```python
from functools import partial
import math

import jax
import jax.numpy as jnp
from jax import lax
from jax.experimental import pallas as pl
from jax.experimental.pallas import tpu as pltpu
from jax.sharding import PartitionSpec as P

HEAD_SIZE = 128
QUERY_PER_GROUP = 8
ADAPTER_RANK = 64
USED = 2

rope_base = 1000000.0

MESH = pl.DeviceIdType.MESH
BLOCK = 2048
LANE_ROWS = 16
SKEW = 2
SHARED_CHUNKS = 9
ALL_CHUNKS = 27
QUARTER = 80


def chip_grid(chips):
    columns = 1
    while 2 * (2 * columns) ** 2 <= chips:
        columns *= 2
    return columns, chips // columns


def path_position(path, x, z, core, columns, rows):
    if path == 0:
        z = z + core * (rows - 1 - 2 * z)
        return x * rows + z + (x % 2) * (rows - 1 - 2 * z)
    x = x + core * (columns - 1 - 2 * x)
    return z * columns + x + (z % 2) * (columns - 1 - 2 * x)


def path_device(path, position, core, columns, rows):
    if path == 0:
        x = position // rows
        z = position % rows
        z = z + (x % 2) * (rows - 1 - 2 * z)
        z = z + core * (rows - 1 - 2 * z)
    else:
        z = position // columns
        x = position % columns
        x = x + (z % 2) * (columns - 1 - 2 * x)
        x = x + core * (columns - 1 - 2 * x)
    return (z * columns + x) * 2 + core


def chunk_place(k, quarter, grp):
    shared = 1 - jnp.minimum(k // SHARED_CHUNKS, 1)
    kk = k - SHARED_CHUNKS * (1 - shared)
    group = kk // 4
    block = kk % 4
    narrow = shared * (group // 2)
    row = (
        QUARTER * quarter
        + LANE_ROWS * group
        + shared * (1 - group // 2) * (32 * grp)
        + narrow * 32
    )
    column = BLOCK * (block + narrow * grp)
    return shared, pl.multiple_of(row, LANE_ROWS), pl.multiple_of(column, BLOCK)


def fetch_kernel(
    seq_size,
    slots,
    ids_ref,
    holder_ref,
    entry_ref,
    x_ref,
    down_ref,
    up_ref,
    out_down_ref,
    out_up_ref,
    shrunk_ref,
    narrow_ref,
    wide_ref,
    own,
    mate_rows,
    moving,
    whole,
    load_sem,
    mate_send,
    mate_recv,
    chain_send,
    chain_recv,
    post_send,
    post_recv,
    cross_send,
    cross_recv,
):
    chips = seq_size // 2
    columns, rows = chip_grid(chips)
    grp = lax.axis_index("grp")
    me = lax.axis_index("seq")
    core = me % 2
    chip = me // 2
    x = chip % columns
    z = chip // columns
    mate = me + 1 - 2 * core
    other = 1 - grp
    positions = [path_position(j, x, z, core, columns, rows) for j in range(2)]

    def device_at(j, position):
        clipped = jnp.clip(position, 0, chips - 1)
        return path_device(j, clipped, core, columns, rows)

    following = [device_at(j, positions[j] + 1) for j in range(2)]
    preceding = [device_at(j, positions[j] - 1) for j in range(2)]

    loads = []
    for q in range(4):
        wide = down_ref.at[0, pl.ds(64 * q, 64)] if q < 3 else out_up_ref.at[0]
        loads.append((wide, own.at[pl.ds(QUARTER * q, 64)]))
        loads.append(
            (
                up_ref.at[0, pl.ds(16 * q, 16)],
                own.at[pl.ds(QUARTER * q + 64, 16), pl.ds(0, 1280)],
            )
        )
        loads.append(
            (
                out_down_ref.at[0, pl.ds(16 * q, 16)],
                own.at[pl.ds(QUARTER * q + 64, 16), pl.ds(1280, 1024)],
            )
        )
    loads = [
        pltpu.make_async_copy(source, target, load_sem.at[i])
        for i, (source, target) in enumerate(loads)
    ]
    for load in loads:
        load.start()
    for q in range(4):
        own[pl.ds(QUARTER * q + 64, 16), pl.ds(2304, 1792)] = jnp.zeros((16, 1792), jnp.bfloat16)

    barrier = pltpu.get_barrier_semaphore()

    def greet(device):
        pl.semaphore_signal(barrier, inc=1, device_id=device, device_id_type=MESH)

    greet((grp, mate))
    greet((other, me))
    greet((other, mate))
    expected = 3
    for j in range(2):

        @pl.when(positions[j] > 0)
        def _():
            greet((grp, preceding[j]))

        @pl.when(positions[j] < chips - 1)
        def _():
            greet((grp, following[j]))

        expected = expected + jnp.minimum(positions[j], 1)
        expected = expected + jnp.minimum(chips - 1 - positions[j], 1)

    rest = jnp.clip(ids_ref[0] + ids_ref[1] - (slots - 1), 0, slots - 1)
    owners = [holder_ref[rest], holder_ref[slots - 1]]
    mine = [jnp.where(owner == me, 1, 0) for owner in owners]
    mates = [jnp.where(owner == mate, 1, 0) for owner in owners]
    ahead = []
    for j in range(2):
        per_path = []
        for owner in owners:
            owner_chip = owner // 2
            place = path_position(
                j, owner_chip % columns, owner_chip // columns, core, columns, rows
            )
            per_path.append(jnp.where(place <= positions[j], 1, 0))
        ahead.append(per_path)
    picked = ids_ref[entry_ref[0]] == slots - 1

    pl.semaphore_wait(barrier, expected)
    for load in loads:
        load.wait()

    def mate_copy(j, order):
        group = [2 * grp, 2 * grp + 1, 4, 2 - 2 * grp, 3 - 2 * grp][order]
        source = 2 * (1 - core) + j
        return pltpu.make_async_remote_copy(
            src_ref=own.at[pl.ds(pl.multiple_of(QUARTER * source + 16 * group, 16), 16)],
            dst_ref=mate_rows.at[pl.ds(pl.multiple_of(QUARTER * j + 16 * group, 16), 16)],
            send_sem=mate_send,
            recv_sem=mate_recv.at[j * 5 + order],
            device_id=(grp, mate),
            device_id_type=MESH,
        )

    for order in range(5):
        for j in range(2):
            mate_copy(j, order).start()

    def chunk(d, j, k):
        return moving.at[d, j, pl.ds(pl.multiple_of(LANE_ROWS * k, LANE_ROWS), LANE_ROWS)]

    def chain_copy(d, j, k):
        return pltpu.make_async_remote_copy(
            src_ref=chunk(d, j, k),
            dst_ref=chunk(d, j, k),
            send_sem=chain_send.at[2 * d + j],
            recv_sem=chain_recv.at[(2 * d + j) * ALL_CHUNKS + k],
            device_id=(grp, following[j] if d == 0 else preceding[j]),
            device_id_type=MESH,
        )

    def post_copy(target, row, column, send_sem, recv_sem):
        piece = whole.at[pl.ds(row, LANE_ROWS), pl.ds(column, BLOCK)]
        return pltpu.make_async_remote_copy(
            src_ref=piece,
            dst_ref=piece,
            send_sem=send_sem,
            recv_sem=recv_sem,
            device_id=target,
            device_id_type=MESH,
        )

    def step(t, carry):
        for at_step, orders in ((0, (0,)), (4, (1,)), (8, (2, 3, 4))):

            @pl.when(t == at_step)
            def _():
                for order in orders:
                    for j in range(2):
                        mate_copy(j, order).wait_recv()

        for j in range(2):
            for d in range(2):
                hops = positions[j] if d == 0 else chips - 1 - positions[j]
                k = t - SKEW * hops

                @pl.when(jnp.logical_and(k >= 0, k < ALL_CHUNKS))
                def _():
                    @pl.when(hops > 0)
                    def _():
                        chain_copy(d, j, k).wait_recv()

                    shared, row, column = chunk_place(k, 2 * core + j, grp)
                    mine_now = mine[0] + shared * (mine[1] - mine[0])
                    mate_now = mates[0] + shared * (mates[1] - mates[0])
                    here = own[pl.ds(row, LANE_ROWS), pl.ds(column, BLOCK)]
                    mate_row = pl.multiple_of(row - 2 * QUARTER * core, LANE_ROWS)
                    there = mate_rows[pl.ds(mate_row, LANE_ROWS), pl.ds(column, BLOCK)]
                    slot = pl.ds(pl.multiple_of(LANE_ROWS * k, LANE_ROWS), LANE_ROWS)
                    passed = moving[d, j, slot]
                    passed = lax.select_n(mate_now == 1, passed, there)
                    moving[d, j, slot] = lax.select_n(mine_now == 1, passed, here)

                    @pl.when(hops < chips - 1)
                    def _():
                        chain_copy(d, j, k).start()

            late = jnp.maximum(positions[j], chips - 1 - positions[j])
            done = t - SKEW * late

            @pl.when(jnp.logical_and(done >= 0, done < ALL_CHUNKS))
            def _():
                shared, row, column = chunk_place(done, 2 * core + j, grp)
                row = pl.multiple_of(row + 4 * QUARTER * shared, LANE_ROWS)
                slot = pl.ds(pl.multiple_of(LANE_ROWS * done, LANE_ROWS), LANE_ROWS)
                ahead_now = ahead[j][0] + shared * (ahead[j][1] - ahead[j][0])
                whole[pl.ds(row, LANE_ROWS), pl.ds(column, BLOCK)] = lax.select_n(
                    ahead_now == 1, moving[1, j, slot], moving[0, j, slot]
                )
                post_copy((grp, mate), row, column, post_send, post_recv).start()

                @pl.when(done < SHARED_CHUNKS)
                def _():
                    post_copy(
                        (other, me), row, column, cross_send.at[0], cross_recv.at[0]
                    ).start()
                    post_copy(
                        (other, mate), row, column, cross_send.at[1], cross_recv.at[1]
                    ).start()

        return carry

    lax.fori_loop(0, ALL_CHUNKS + SKEW * (chips - 1), step, 0)

    def drain(ref, sem):
        pltpu.make_async_copy(ref, ref, sem).wait()

    both = moving.at[0]
    cross = moving.at[0, :, pl.ds(0, LANE_ROWS * SHARED_CHUNKS)]
    drain(both, post_recv)
    for i in range(2):
        drain(cross, cross_recv.at[i])

    total = jnp.zeros((x_ref.shape[0], 3 * ADAPTER_RANK), jnp.float32)

    def shrink(block, total):
        at = pl.ds(pl.multiple_of(block * BLOCK, BLOCK), BLOCK)
        parts = [
            lax.select_n(
                picked,
                whole[pl.ds(QUARTER * q, 64), at],
                whole[pl.ds(QUARTER * (4 + q), 64), at],
            )
            for q in range(3)
        ]
        return total + lax.dot_general(
            x_ref[:, at],
            jnp.concatenate(parts, 0),
            (((1,), (1,)), ((), ())),
            preferred_element_type=jnp.float32,
        )

    total = lax.fori_loop(0, x_ref.shape[1] // BLOCK, shrink, total)
    shrunk_ref[...] = total.astype(jnp.bfloat16)
    for q in range(4):
        at = pl.ds(0, 2304)
        narrow_ref[pl.ds(16 * q, 16), :] = lax.select_n(
            picked,
            whole[pl.ds(QUARTER * q + 64, 16), at],
            whole[pl.ds(QUARTER * (4 + q) + 64, 16), at],
        )

    def copy_wide(block, carry):
        at = pl.ds(pl.multiple_of(block * BLOCK, BLOCK), BLOCK)
        wide_ref[:, at] = lax.select_n(
            picked,
            whole[pl.ds(QUARTER * 3, 64), at],
            whole[pl.ds(QUARTER * 7, 64), at],
        )
        return carry

    lax.fori_loop(0, wide_ref.shape[1] // BLOCK, copy_wide, 0)

    drain(mate_rows, mate_send)
    for j in range(2):
        for d in range(2):
            hops = positions[j] if d == 0 else chips - 1 - positions[j]

            @pl.when(hops < chips - 1)
            def _():
                drain(moving.at[d, j], chain_send.at[2 * d + j])

    drain(both, post_send)
    for i in range(2):
        drain(cross, cross_send.at[i])


def rope_tables(positions, head_width):
    half_width = head_width // 2
    frequency = jnp.exp(
        jnp.arange(half_width, dtype=jnp.float32) * (-2.0 * math.log(rope_base) / head_width)
    )
    angles = positions.astype(jnp.float32)[:, None] * frequency[None, :]
    return (jnp.cos(angles), jnp.sin(angles))


def attend_kernel(
    seq_size,
    shrunk_ref,
    narrow_ref,
    base_ref,
    cosine_ref,
    sine_ref,
    attended_ref,
    out_shrunk_ref,
    pairs,
    queries,
    maxima,
    totals,
    summed,
    line_send,
    cross_send,
    mate_send,
    recv,
):
    columns, rows = chip_grid(seq_size // 2)
    grp = lax.axis_index("grp")
    me = lax.axis_index("seq")
    core = me % 2
    x = (me // 2) % columns
    z = me // (2 * columns)
    mate = me + 1 - 2 * core
    tokens = base_ref.shape[0]
    query_width = QUERY_PER_GROUP * HEAD_SIZE
    level = 2 * columns * tokens

    def device(z, x, core):
        return (z * columns + x) * 2 + core

    barrier = pltpu.get_barrier_semaphore()

    def greet(other):
        pl.semaphore_signal(barrier, inc=1, device_id=(grp, other), device_id_type=MESH)

    def greet_line(i, carry):
        greet(device((z + i) % rows, x, core))
        return carry

    lax.fori_loop(1, rows, greet_line, 0)
    for i in range(1, columns):
        greet(device(z, (x + i) % columns, core))
    greet(mate)

    rank = ADAPTER_RANK

    def project(first, width, member):
        return base_ref[:, pl.ds(first, width)].astype(jnp.float32) + jnp.dot(
            shrunk_ref[:, member * rank : (member + 1) * rank],
            narrow_ref[:, pl.ds(first, width)],
            preferred_element_type=jnp.float32,
        )

    cosine = cosine_ref[...]
    sine = sine_ref[...]

    def turn(vectors):
        swapped = pltpu.roll(vectors, HEAD_SIZE // 2, 1)
        return (vectors * cosine + swapped * sine).astype(jnp.bfloat16)

    def rows_of(owner):
        return pl.ds(pl.multiple_of(owner * tokens, tokens), tokens)

    pairs[rows_of(me), pl.ds(0, HEAD_SIZE)] = turn(project(query_width, HEAD_SIZE, 1))
    pairs[rows_of(me), pl.ds(HEAD_SIZE, HEAD_SIZE)] = project(
        query_width + HEAD_SIZE, HEAD_SIZE, 2
    ).astype(jnp.bfloat16)

    pl.semaphore_wait(barrier, rows - 1 + columns - 1 + 1)

    def send(owner, target, send_sem):
        return pltpu.make_async_remote_copy(
            src_ref=pairs.at[rows_of(owner)],
            dst_ref=pairs.at[rows_of(owner)],
            send_sem=send_sem,
            recv_sem=recv.at[owner],
            device_id=(grp, target),
            device_id_type=MESH,
        )

    def to_line(later):
        return send(me, device(later, x, core), line_send.at[later])

    def to_row(deep, i):
        return send(
            device(deep, x, core),
            device(z, (x + i) % columns, core),
            cross_send.at[deep * columns + i],
        )

    def to_mate(deep, i):
        i = (x + i) % columns
        return send(device(deep, i, core), mate, mate_send.at[deep * columns + i])

    def await_pair(owner):
        piece = pairs.at[rows_of(owner)]
        pltpu.make_async_copy(piece, piece, recv.at[owner]).wait()

    def relay(deep):
        for i in range(1, columns):
            to_row(deep, i).start()
        to_mate(deep, 0).start()

    def start_line(later, carry):
        to_line(later).start()
        return carry

    relay(z)
    lax.fori_loop(z + 1, rows, start_line, 0)

    for h in range(QUERY_PER_GROUP):
        queries[pl.ds(h * tokens, tokens), :] = turn(project(h * HEAD_SIZE, HEAD_SIZE, 0))
    maxima[...] = jnp.full_like(maxima, -1e30)
    totals[...] = jnp.zeros_like(totals)
    summed[...] = jnp.zeros_like(summed)

    together = 2 * tokens

    def one_level(o, carry):
        deep = z - o

        @pl.when(o < z)
        def _():
            await_pair(device(deep - 1, x, core))
            relay(deep - 1)

        for i in range(1, columns):
            await_pair(device(deep, (x + i) % columns, core))
            to_mate(deep, i).start()
        for i in range(columns):
            await_pair(device(deep, i, 1 - core))

        at = pl.ds(pl.multiple_of(deep * level, level), level)
        keys = pairs[at, pl.ds(0, HEAD_SIZE)]
        values = pairs[at, pl.ds(HEAD_SIZE, HEAD_SIZE)]
        key_place = deep * level + lax.broadcasted_iota(jnp.int32, (together, level), 1)
        row_place = me * tokens + lax.broadcasted_iota(jnp.int32, (together, level), 0) % tokens
        visible = key_place <= row_place
        for first in range(0, QUERY_PER_GROUP * tokens, together):
            here = pl.ds(first, together)
            scores = lax.dot_general(
                queries[here, :],
                keys,
                (((1,), (1,)), ((), ())),
                preferred_element_type=jnp.float32,
            ) * HEAD_SIZE ** (-0.5)
            scores = jnp.where(visible, scores, -1e30)
            before = maxima[here, :]
            now = jnp.maximum(before, jnp.max(scores, 1, keepdims=True))
            weights = jnp.where(visible, jnp.exp(scores - now), 0.0)
            rescale = jnp.exp(before - now)
            maxima[here, :] = now
            totals[here, :] = totals[here, :] * rescale + jnp.sum(weights, 1, keepdims=True)
            summed[here, :] = summed[here, :] * rescale + jnp.dot(
                weights.astype(jnp.bfloat16), values, preferred_element_type=jnp.float32
            )
        return carry

    lax.fori_loop(0, z + 1, one_level, 0)

    for h in range(QUERY_PER_GROUP):
        here = pl.ds(h * tokens, tokens)
        attended_ref[:, pl.ds(h * HEAD_SIZE, HEAD_SIZE)] = (
            summed[here, :] / totals[here, :]
        ).astype(jnp.bfloat16)
    out_shrunk_ref[...] = lax.dot_general(
        attended_ref[...],
        narrow_ref[:, pl.ds(query_width + 2 * HEAD_SIZE, query_width)],
        (((1,), (1,)), ((), ())),
        preferred_element_type=jnp.float32,
    ).astype(jnp.bfloat16)

    def end_line(later, carry):
        to_line(later).wait_send()
        return carry

    lax.fori_loop(z + 1, rows, end_line, 0)

    def end_level(deep, carry):
        for i in range(1, columns):
            to_row(deep, i).wait_send()
        for i in range(columns):
            to_mate(deep, i).wait_send()
        return carry

    lax.fori_loop(0, z + 1, end_level, 0)


def shards(
    seq_size,
    normed_input,
    base_projection_weight,
    adapter_down_pool,
    adapter_up_pool,
    output_down_pool,
    output_up_pool,
    request_adapter_ids,
    holder,
    segment_adapter_entry,
):
    tok_rows, width = normed_input.shape
    query_width = QUERY_PER_GROUP * HEAD_SIZE
    slots = holder.shape[0]
    in_smem = pl.BlockSpec(memory_space=pltpu.SMEM)
    in_vmem = pl.BlockSpec(memory_space=pltpu.VMEM)
    in_any = pl.BlockSpec(memory_space=pl.ANY)
    bf16 = jnp.bfloat16
    reduced_rank_rows, narrow, out_up = pl.pallas_call(
        partial(fetch_kernel, seq_size, slots),
        out_shape=(
            jax.ShapeDtypeStruct((tok_rows, 3 * ADAPTER_RANK), bf16),
            jax.ShapeDtypeStruct((ADAPTER_RANK, 2304), bf16),
            jax.ShapeDtypeStruct((ADAPTER_RANK, width), bf16),
        ),
        in_specs=[in_smem] * 3 + [in_vmem] + [in_any] * 4,
        out_specs=(in_vmem, in_vmem, in_vmem),
        scratch_shapes=[
            pltpu.VMEM((4 * QUARTER, width), bf16),
            pltpu.VMEM((2 * QUARTER, width), bf16),
            pltpu.VMEM((2, 2, LANE_ROWS * ALL_CHUNKS, BLOCK), bf16),
            pltpu.VMEM((8 * QUARTER, width), bf16),
            pltpu.SemaphoreType.DMA((12,)),
            pltpu.SemaphoreType.DMA,
            pltpu.SemaphoreType.DMA((10,)),
            pltpu.SemaphoreType.DMA((4,)),
            pltpu.SemaphoreType.DMA((4 * ALL_CHUNKS,)),
            pltpu.SemaphoreType.DMA,
            pltpu.SemaphoreType.DMA,
            pltpu.SemaphoreType.DMA((2,)),
            pltpu.SemaphoreType.DMA((2,)),
        ],
        compiler_params=pltpu.CompilerParams(
            collective_id=0, has_side_effects=True, vmem_limit_bytes=60 * 1024 * 1024
        ),
        name="fetch",
    )(
        request_adapter_ids,
        holder,
        segment_adapter_entry,
        normed_input,
        adapter_down_pool,
        adapter_up_pool,
        output_down_pool,
        output_up_pool,
    )
    positions = lax.axis_index("seq") * tok_rows + jnp.arange(tok_rows, dtype=jnp.int32)
    cosine, sine = rope_tables(positions, HEAD_SIZE)
    columns, rows = chip_grid(seq_size // 2)
    heads = QUERY_PER_GROUP * tok_rows
    attended, reduced_out_rows = pl.pallas_call(
        partial(attend_kernel, seq_size),
        out_shape=(
            jax.ShapeDtypeStruct((tok_rows, query_width), bf16),
            jax.ShapeDtypeStruct((tok_rows, ADAPTER_RANK), bf16),
        ),
        in_specs=[in_vmem] * 5,
        out_specs=(in_vmem, in_vmem),
        scratch_shapes=[
            pltpu.VMEM((seq_size * tok_rows, 2 * HEAD_SIZE), bf16),
            pltpu.VMEM((heads, HEAD_SIZE), bf16),
            pltpu.VMEM((heads, 1), jnp.float32),
            pltpu.VMEM((heads, 1), jnp.float32),
            pltpu.VMEM((heads, HEAD_SIZE), jnp.float32),
            pltpu.SemaphoreType.DMA((rows,)),
            pltpu.SemaphoreType.DMA((rows * columns,)),
            pltpu.SemaphoreType.DMA((rows * columns,)),
            pltpu.SemaphoreType.DMA((seq_size,)),
        ],
        compiler_params=pltpu.CompilerParams(
            collective_id=1, has_side_effects=True, vmem_limit_bytes=40 * 1024 * 1024
        ),
        name="attend",
    )(
        reduced_rank_rows,
        narrow,
        base_projection_weight,
        jnp.concatenate([cosine, cosine], 1),
        jnp.concatenate([-sine, sine], 1),
    )
    out_rows = jnp.dot(reduced_out_rows, out_up, preferred_element_type=jnp.float32).astype(
        jnp.bfloat16
    )
    return (attended, out_rows)


def solution(mesh):
    in_specs = (
        P(("grp", "seq"), None),
        P(("grp", "seq"), None),
        P("seq", None, None),
        P("seq", None, None),
        P("seq", None, None),
        P("seq", None, None),
        P("grp"),
        P(),
        P(("grp", "seq")),
    )
    out_specs = (P(("grp", "seq"), None), P(("grp", "seq"), None))
    return jax.shard_map(
        partial(shards, mesh.shape["seq"]),
        mesh=mesh,
        in_specs=in_specs,
        out_specs=out_specs,
        check_vma=False,
    )
```

```python
from functools import partial
import math

import jax
import jax.numpy as jnp
from jax import lax
from jax.experimental import pallas as pl
from jax.experimental.pallas import tpu as pltpu
from jax.sharding import PartitionSpec as P

HEAD_SIZE = 128
QUERY_PER_GROUP = 8
ADAPTER_RANK = 64
USED = 2

rope_base = 1000000.0

MESH = pl.DeviceIdType.MESH
BLOCK = 2048
LANE_ROWS = 16
SKEW = 2
SHARED_CHUNKS = 9
ALL_CHUNKS = 27
QUARTER = 80


def chip_grid(chips):
    columns = 1
    while 2 * (2 * columns) ** 2 <= chips:
        columns *= 2
    return columns, chips // columns


def path_position(path, x, z, core, columns, rows):
    if path == 0:
        z = z + core * (rows - 1 - 2 * z)
        return x * rows + z + (x % 2) * (rows - 1 - 2 * z)
    x = x + core * (columns - 1 - 2 * x)
    return z * columns + x + (z % 2) * (columns - 1 - 2 * x)


def path_device(path, position, core, columns, rows):
    if path == 0:
        x = position // rows
        z = position % rows
        z = z + (x % 2) * (rows - 1 - 2 * z)
        z = z + core * (rows - 1 - 2 * z)
    else:
        z = position // columns
        x = position % columns
        x = x + (z % 2) * (columns - 1 - 2 * x)
        x = x + core * (columns - 1 - 2 * x)
    return (z * columns + x) * 2 + core


def chunk_place(k, quarter, grp):
    shared = 1 - jnp.minimum(k // SHARED_CHUNKS, 1)
    kk = k - SHARED_CHUNKS * (1 - shared)
    group = kk // 4
    block = kk % 4
    narrow = shared * (group // 2)
    row = (
        QUARTER * quarter
        + LANE_ROWS * group
        + shared * (1 - group // 2) * (32 * grp)
        + narrow * 32
    )
    column = BLOCK * (block + narrow * grp)
    return shared, pl.multiple_of(row, LANE_ROWS), pl.multiple_of(column, BLOCK)


def fetch_kernel(
    seq_size,
    slots,
    ids_ref,
    holder_ref,
    entry_ref,
    x_ref,
    down_ref,
    up_ref,
    out_down_ref,
    out_up_ref,
    shrunk_ref,
    narrow_ref,
    wide_ref,
    own,
    mate_rows,
    moving,
    whole,
    x_rows,
    load_sem,
    mate_send,
    mate_recv,
    chain_send,
    chain_recv,
    post_send,
    post_recv,
    cross_send,
    cross_recv,
):
    chips = seq_size // 2
    columns, rows = chip_grid(chips)
    grp = lax.axis_index("grp")
    me = lax.axis_index("seq")
    core = me % 2
    chip = me // 2
    x = chip % columns
    z = chip // columns
    mate = me + 1 - 2 * core
    other = 1 - grp
    positions = [path_position(j, x, z, core, columns, rows) for j in range(2)]

    def device_at(j, position):
        clipped = jnp.clip(position, 0, chips - 1)
        return path_device(j, clipped, core, columns, rows)

    following = [device_at(j, positions[j] + 1) for j in range(2)]
    preceding = [device_at(j, positions[j] - 1) for j in range(2)]

    loads = []
    for q in range(4):
        wide = down_ref.at[0, pl.ds(64 * q, 64)] if q < 3 else out_up_ref.at[0]
        loads.append((wide, own.at[pl.ds(QUARTER * q, 64)]))
        loads.append(
            (
                up_ref.at[0, pl.ds(16 * q, 16)],
                own.at[pl.ds(QUARTER * q + 64, 16), pl.ds(0, 1280)],
            )
        )
        loads.append(
            (
                out_down_ref.at[0, pl.ds(16 * q, 16)],
                own.at[pl.ds(QUARTER * q + 64, 16), pl.ds(1280, 1024)],
            )
        )
    loads = [
        pltpu.make_async_copy(source, target, load_sem.at[i])
        for i, (source, target) in enumerate(loads)
    ]
    for load in loads:
        load.start()
    x_load = pltpu.make_async_copy(x_ref, x_rows, load_sem.at[len(loads)])
    x_load.start()
    for q in range(4):
        own[pl.ds(QUARTER * q + 64, 16), pl.ds(2304, 1792)] = jnp.zeros((16, 1792), jnp.bfloat16)

    barrier = pltpu.get_barrier_semaphore()

    def greet(device):
        pl.semaphore_signal(barrier, inc=1, device_id=device, device_id_type=MESH)

    greet((grp, mate))
    greet((other, me))
    greet((other, mate))
    expected = 3
    for j in range(2):

        @pl.when(positions[j] > 0)
        def _():
            greet((grp, preceding[j]))

        @pl.when(positions[j] < chips - 1)
        def _():
            greet((grp, following[j]))

        expected = expected + jnp.minimum(positions[j], 1)
        expected = expected + jnp.minimum(chips - 1 - positions[j], 1)

    rest = jnp.clip(ids_ref[0] + ids_ref[1] - (slots - 1), 0, slots - 1)
    owners = [holder_ref[rest], holder_ref[slots - 1]]
    mine = [jnp.where(owner == me, 1, 0) for owner in owners]
    mates = [jnp.where(owner == mate, 1, 0) for owner in owners]
    ahead = []
    for j in range(2):
        per_path = []
        for owner in owners:
            owner_chip = owner // 2
            place = path_position(
                j, owner_chip % columns, owner_chip // columns, core, columns, rows
            )
            per_path.append(jnp.where(place <= positions[j], 1, 0))
        ahead.append(per_path)
    picked = ids_ref[entry_ref[0]] == slots - 1

    pl.semaphore_wait(barrier, expected)
    for load in loads:
        load.wait()

    def mate_copy(j, order):
        group = [2 * grp, 2 * grp + 1, 4, 2 - 2 * grp, 3 - 2 * grp][order]
        source = 2 * (1 - core) + j
        return pltpu.make_async_remote_copy(
            src_ref=own.at[pl.ds(pl.multiple_of(QUARTER * source + 16 * group, 16), 16)],
            dst_ref=mate_rows.at[pl.ds(pl.multiple_of(QUARTER * j + 16 * group, 16), 16)],
            send_sem=mate_send,
            recv_sem=mate_recv.at[j * 5 + order],
            device_id=(grp, mate),
            device_id_type=MESH,
        )

    for order in range(5):
        for j in range(2):
            mate_copy(j, order).start()

    def chunk(d, j, k):
        return moving.at[d, j, pl.ds(pl.multiple_of(LANE_ROWS * k, LANE_ROWS), LANE_ROWS)]

    def chain_copy(d, j, k):
        return pltpu.make_async_remote_copy(
            src_ref=chunk(d, j, k),
            dst_ref=chunk(d, j, k),
            send_sem=chain_send.at[2 * d + j],
            recv_sem=chain_recv.at[(2 * d + j) * ALL_CHUNKS + k],
            device_id=(grp, following[j] if d == 0 else preceding[j]),
            device_id_type=MESH,
        )

    def post_copy(target, row, column, send_sem, recv_sem):
        piece = whole.at[pl.ds(row, LANE_ROWS), pl.ds(column, BLOCK)]
        return pltpu.make_async_remote_copy(
            src_ref=piece,
            dst_ref=piece,
            send_sem=send_sem,
            recv_sem=recv_sem,
            device_id=target,
            device_id_type=MESH,
        )

    def step(t, carry):
        for at_step, orders in ((0, (0,)), (4, (1,)), (8, (2, 3, 4))):

            @pl.when(t == at_step)
            def _():
                for order in orders:
                    for j in range(2):
                        mate_copy(j, order).wait_recv()

        for j in range(2):
            for d in range(2):
                hops = positions[j] if d == 0 else chips - 1 - positions[j]
                k = t - SKEW * hops

                @pl.when(jnp.logical_and(k >= 0, k < ALL_CHUNKS))
                def _():
                    @pl.when(hops > 0)
                    def _():
                        chain_copy(d, j, k).wait_recv()

                    shared, row, column = chunk_place(k, 2 * core + j, grp)
                    mine_now = mine[0] + shared * (mine[1] - mine[0])
                    mate_now = mates[0] + shared * (mates[1] - mates[0])
                    here = own[pl.ds(row, LANE_ROWS), pl.ds(column, BLOCK)]
                    mate_row = pl.multiple_of(row - 2 * QUARTER * core, LANE_ROWS)
                    there = mate_rows[pl.ds(mate_row, LANE_ROWS), pl.ds(column, BLOCK)]
                    slot = pl.ds(pl.multiple_of(LANE_ROWS * k, LANE_ROWS), LANE_ROWS)
                    passed = moving[d, j, slot]
                    passed = lax.select_n(mate_now == 1, passed, there)
                    moving[d, j, slot] = lax.select_n(mine_now == 1, passed, here)

                    @pl.when(hops < chips - 1)
                    def _():
                        chain_copy(d, j, k).start()

            late = jnp.maximum(positions[j], chips - 1 - positions[j])
            done = t - SKEW * late

            @pl.when(jnp.logical_and(done >= 0, done < ALL_CHUNKS))
            def _():
                shared, row, column = chunk_place(done, 2 * core + j, grp)
                row = pl.multiple_of(row + 4 * QUARTER * shared, LANE_ROWS)
                slot = pl.ds(pl.multiple_of(LANE_ROWS * done, LANE_ROWS), LANE_ROWS)
                ahead_now = ahead[j][0] + shared * (ahead[j][1] - ahead[j][0])
                whole[pl.ds(row, LANE_ROWS), pl.ds(column, BLOCK)] = lax.select_n(
                    ahead_now == 1, moving[1, j, slot], moving[0, j, slot]
                )
                post_copy((grp, mate), row, column, post_send, post_recv).start()

                @pl.when(done < SHARED_CHUNKS)
                def _():
                    post_copy(
                        (other, me), row, column, cross_send.at[0], cross_recv.at[0]
                    ).start()
                    post_copy(
                        (other, mate), row, column, cross_send.at[1], cross_recv.at[1]
                    ).start()

        return carry

    lax.fori_loop(0, ALL_CHUNKS + SKEW * (chips - 1), step, 0)

    def drain(ref, sem):
        pltpu.make_async_copy(ref, ref, sem).wait()

    both = moving.at[0]
    cross = moving.at[0, :, pl.ds(0, LANE_ROWS * SHARED_CHUNKS)]
    drain(both, post_recv)
    for i in range(2):
        drain(cross, cross_recv.at[i])

    x_load.wait()
    total = jnp.zeros((x_ref.shape[0], 3 * ADAPTER_RANK), jnp.float32)

    def shrink(block, total):
        at = pl.ds(pl.multiple_of(block * BLOCK, BLOCK), BLOCK)
        parts = [
            lax.select_n(
                picked,
                whole[pl.ds(QUARTER * q, 64), at],
                whole[pl.ds(QUARTER * (4 + q), 64), at],
            )
            for q in range(3)
        ]
        return total + lax.dot_general(
            x_rows[:, at],
            jnp.concatenate(parts, 0),
            (((1,), (1,)), ((), ())),
            preferred_element_type=jnp.float32,
        )

    total = lax.fori_loop(0, x_ref.shape[1] // BLOCK, shrink, total)
    shrunk_ref[...] = total.astype(jnp.bfloat16)
    for q in range(4):
        at = pl.ds(0, 2304)
        narrow_ref[pl.ds(16 * q, 16), :] = lax.select_n(
            picked,
            whole[pl.ds(QUARTER * q + 64, 16), at],
            whole[pl.ds(QUARTER * (4 + q) + 64, 16), at],
        )

    def copy_wide(block, carry):
        at = pl.ds(pl.multiple_of(block * BLOCK, BLOCK), BLOCK)
        wide_ref[:, at] = lax.select_n(
            picked,
            whole[pl.ds(QUARTER * 3, 64), at],
            whole[pl.ds(QUARTER * 7, 64), at],
        )
        return carry

    lax.fori_loop(0, wide_ref.shape[1] // BLOCK, copy_wide, 0)

    drain(mate_rows, mate_send)
    for j in range(2):
        for d in range(2):
            hops = positions[j] if d == 0 else chips - 1 - positions[j]

            @pl.when(hops < chips - 1)
            def _():
                drain(moving.at[d, j], chain_send.at[2 * d + j])

    drain(both, post_send)
    for i in range(2):
        drain(cross, cross_send.at[i])


def rope_tables(positions, head_width):
    half_width = head_width // 2
    frequency = jnp.exp(
        jnp.arange(half_width, dtype=jnp.float32) * (-2.0 * math.log(rope_base) / head_width)
    )
    angles = positions.astype(jnp.float32)[:, None] * frequency[None, :]
    return (jnp.cos(angles), jnp.sin(angles))


def attend_kernel(
    seq_size,
    shrunk_ref,
    narrow_ref,
    base_ref,
    cosine_ref,
    sine_ref,
    attended_ref,
    out_shrunk_ref,
    pairs,
    queries,
    maxima,
    totals,
    summed,
    line_send,
    level_send,
    recv,
):
    columns, rows = chip_grid(seq_size // 2)
    grp = lax.axis_index("grp")
    me = lax.axis_index("seq")
    core = me % 2
    x = (me // 2) % columns
    z = me // (2 * columns)
    peers = 2 * columns
    tokens = base_ref.shape[0]
    query_width = QUERY_PER_GROUP * HEAD_SIZE
    level = peers * tokens

    def device(z, x, core):
        return (z * columns + x) * 2 + core

    barrier = pltpu.get_barrier_semaphore()

    def greet(other):
        pl.semaphore_signal(barrier, inc=1, device_id=(grp, other), device_id_type=MESH)

    def greet_line(i, carry):
        greet(device((z + i) % rows, x, core))
        return carry

    lax.fori_loop(1, rows, greet_line, 0)
    for i in range(1, peers):
        greet(z * peers + (me + i) % peers)

    rank = ADAPTER_RANK

    def project(first, width, member):
        return base_ref[:, pl.ds(first, width)].astype(jnp.float32) + jnp.dot(
            shrunk_ref[:, member * rank : (member + 1) * rank],
            narrow_ref[:, pl.ds(first, width)],
            preferred_element_type=jnp.float32,
        )

    cosine = cosine_ref[...]
    sine = sine_ref[...]

    def turn(vectors):
        swapped = pltpu.roll(vectors, HEAD_SIZE // 2, 1)
        return (vectors * cosine + swapped * sine).astype(jnp.bfloat16)

    def rows_of(owner):
        return pl.ds(pl.multiple_of(owner * tokens, tokens), tokens)

    pairs[rows_of(me), pl.ds(0, HEAD_SIZE)] = turn(project(query_width, HEAD_SIZE, 1))
    pairs[rows_of(me), pl.ds(HEAD_SIZE, HEAD_SIZE)] = project(
        query_width + HEAD_SIZE, HEAD_SIZE, 2
    ).astype(jnp.bfloat16)

    pl.semaphore_wait(barrier, rows - 1 + peers - 1)

    def send(owner, target, send_sem):
        return pltpu.make_async_remote_copy(
            src_ref=pairs.at[rows_of(owner)],
            dst_ref=pairs.at[rows_of(owner)],
            send_sem=send_sem,
            recv_sem=recv.at[owner],
            device_id=(grp, target),
            device_id_type=MESH,
        )

    def to_line(later):
        return send(me, device(later, x, core), line_send.at[later])

    def to_peer(deep, i):
        return send(
            device(deep, x, core),
            z * peers + (me + i) % peers,
            level_send.at[deep * peers + i],
        )

    def await_pair(owner):
        piece = pairs.at[rows_of(owner)]
        pltpu.make_async_copy(piece, piece, recv.at[owner]).wait()

    def relay(deep):
        for i in range(1, peers):
            to_peer(deep, i).start()

    def start_line(later, carry):
        to_line(later).start()
        return carry

    lax.fori_loop(z + 1, rows, start_line, 0)
    relay(z)

    for h in range(QUERY_PER_GROUP):
        queries[pl.ds(h * tokens, tokens), :] = turn(project(h * HEAD_SIZE, HEAD_SIZE, 0))
    maxima[...] = jnp.full_like(maxima, -1e30)
    totals[...] = jnp.zeros_like(totals)
    summed[...] = jnp.zeros_like(summed)

    together = 2 * tokens

    def one_level(o, carry):
        deep = z - o

        @pl.when(o < z)
        def _():
            await_pair(device(deep - 1, x, core))
            relay(deep - 1)

        for i in range(1, peers):
            await_pair(deep * peers + (me + i) % peers)

        at = pl.ds(pl.multiple_of(deep * level, level), level)
        keys = pairs[at, pl.ds(0, HEAD_SIZE)]
        values = pairs[at, pl.ds(HEAD_SIZE, HEAD_SIZE)]
        key_place = deep * level + lax.broadcasted_iota(jnp.int32, (together, level), 1)
        row_place = me * tokens + lax.broadcasted_iota(jnp.int32, (together, level), 0) % tokens
        visible = key_place <= row_place
        for first in range(0, QUERY_PER_GROUP * tokens, together):
            here = pl.ds(first, together)
            scores = lax.dot_general(
                queries[here, :],
                keys,
                (((1,), (1,)), ((), ())),
                preferred_element_type=jnp.float32,
            ) * HEAD_SIZE ** (-0.5)
            scores = jnp.where(visible, scores, -1e30)
            before = maxima[here, :]
            now = jnp.maximum(before, jnp.max(scores, 1, keepdims=True))
            weights = jnp.where(visible, jnp.exp(scores - now), 0.0)
            rescale = jnp.exp(before - now)
            maxima[here, :] = now
            totals[here, :] = totals[here, :] * rescale + jnp.sum(weights, 1, keepdims=True)
            summed[here, :] = summed[here, :] * rescale + jnp.dot(
                weights.astype(jnp.bfloat16), values, preferred_element_type=jnp.float32
            )
        return carry

    lax.fori_loop(0, z + 1, one_level, 0)

    for h in range(QUERY_PER_GROUP):
        here = pl.ds(h * tokens, tokens)
        attended_ref[:, pl.ds(h * HEAD_SIZE, HEAD_SIZE)] = (
            summed[here, :] / totals[here, :]
        ).astype(jnp.bfloat16)
    out_shrunk_ref[...] = lax.dot_general(
        attended_ref[...],
        narrow_ref[:, pl.ds(query_width + 2 * HEAD_SIZE, query_width)],
        (((1,), (1,)), ((), ())),
        preferred_element_type=jnp.float32,
    ).astype(jnp.bfloat16)

    def end_line(later, carry):
        to_line(later).wait_send()
        return carry

    lax.fori_loop(z + 1, rows, end_line, 0)

    def end_level(deep, carry):
        for i in range(1, peers):
            to_peer(deep, i).wait_send()
        return carry

    lax.fori_loop(0, z + 1, end_level, 0)


def shards(
    seq_size,
    normed_input,
    base_projection_weight,
    adapter_down_pool,
    adapter_up_pool,
    output_down_pool,
    output_up_pool,
    request_adapter_ids,
    holder,
    segment_adapter_entry,
):
    tok_rows, width = normed_input.shape
    query_width = QUERY_PER_GROUP * HEAD_SIZE
    slots = holder.shape[0]
    in_smem = pl.BlockSpec(memory_space=pltpu.SMEM)
    in_vmem = pl.BlockSpec(memory_space=pltpu.VMEM)
    in_any = pl.BlockSpec(memory_space=pl.ANY)
    bf16 = jnp.bfloat16
    reduced_rank_rows, narrow, out_up = pl.pallas_call(
        partial(fetch_kernel, seq_size, slots),
        out_shape=(
            jax.ShapeDtypeStruct((tok_rows, 3 * ADAPTER_RANK), bf16),
            jax.ShapeDtypeStruct((ADAPTER_RANK, 2304), bf16),
            jax.ShapeDtypeStruct((ADAPTER_RANK, width), bf16),
        ),
        in_specs=[in_smem] * 3 + [in_any] * 5,
        out_specs=(in_vmem, in_vmem, in_vmem),
        scratch_shapes=[
            pltpu.VMEM((4 * QUARTER, width), bf16),
            pltpu.VMEM((2 * QUARTER, width), bf16),
            pltpu.VMEM((2, 2, LANE_ROWS * ALL_CHUNKS, BLOCK), bf16),
            pltpu.VMEM((8 * QUARTER, width), bf16),
            pltpu.VMEM((tok_rows, width), bf16),
            pltpu.SemaphoreType.DMA((13,)),
            pltpu.SemaphoreType.DMA,
            pltpu.SemaphoreType.DMA((10,)),
            pltpu.SemaphoreType.DMA((4,)),
            pltpu.SemaphoreType.DMA((4 * ALL_CHUNKS,)),
            pltpu.SemaphoreType.DMA,
            pltpu.SemaphoreType.DMA,
            pltpu.SemaphoreType.DMA((2,)),
            pltpu.SemaphoreType.DMA((2,)),
        ],
        compiler_params=pltpu.CompilerParams(
            collective_id=0, has_side_effects=True, vmem_limit_bytes=60 * 1024 * 1024
        ),
        name="fetch",
    )(
        request_adapter_ids,
        holder,
        segment_adapter_entry,
        normed_input,
        adapter_down_pool,
        adapter_up_pool,
        output_down_pool,
        output_up_pool,
    )
    positions = lax.axis_index("seq") * tok_rows + jnp.arange(tok_rows, dtype=jnp.int32)
    cosine, sine = rope_tables(positions, HEAD_SIZE)
    columns, rows = chip_grid(seq_size // 2)
    heads = QUERY_PER_GROUP * tok_rows
    attended, reduced_out_rows = pl.pallas_call(
        partial(attend_kernel, seq_size),
        out_shape=(
            jax.ShapeDtypeStruct((tok_rows, query_width), bf16),
            jax.ShapeDtypeStruct((tok_rows, ADAPTER_RANK), bf16),
        ),
        in_specs=[in_vmem] * 5,
        out_specs=(in_vmem, in_vmem),
        scratch_shapes=[
            pltpu.VMEM((seq_size * tok_rows, 2 * HEAD_SIZE), bf16),
            pltpu.VMEM((heads, HEAD_SIZE), bf16),
            pltpu.VMEM((heads, 1), jnp.float32),
            pltpu.VMEM((heads, 1), jnp.float32),
            pltpu.VMEM((heads, HEAD_SIZE), jnp.float32),
            pltpu.SemaphoreType.DMA((rows,)),
            pltpu.SemaphoreType.DMA((seq_size,)),
            pltpu.SemaphoreType.DMA((seq_size,)),
        ],
        compiler_params=pltpu.CompilerParams(
            collective_id=1, has_side_effects=True, vmem_limit_bytes=40 * 1024 * 1024
        ),
        name="attend",
    )(
        reduced_rank_rows,
        narrow,
        base_projection_weight,
        jnp.concatenate([cosine, cosine], 1),
        jnp.concatenate([-sine, sine], 1),
    )
    out_rows = jnp.dot(reduced_out_rows, out_up, preferred_element_type=jnp.float32).astype(
        jnp.bfloat16
    )
    return (attended, out_rows)


def solution(mesh):
    in_specs = (
        P(("grp", "seq"), None),
        P(("grp", "seq"), None),
        P("seq", None, None),
        P("seq", None, None),
        P("seq", None, None),
        P("seq", None, None),
        P("grp"),
        P(),
        P(("grp", "seq")),
    )
    out_specs = (P(("grp", "seq"), None), P(("grp", "seq"), None))
    return jax.shard_map(
        partial(shards, mesh.shape["seq"]),
        mesh=mesh,
        in_specs=in_specs,
        out_specs=out_specs,
        check_vma=False,
    )
```
